768 devices in a mesh: row: 64 (over y, x, core), col: 12 (over z).
Axes of the slice: x: 4, y: 8, z: 12, core: 2. Of those that a mesh axis runs over, the one named last changes fastest.
Arguments:
- a_blocks: bfloat16 [1024, 1536, 128], P('row', 'col'), may hold values from -6 to 6
- b_blocks: bfloat16 [1024, 1536, 128], P('row', 'col'), may hold values from -0.125 to 0.125
- pair_a: int32 [3072, 192], P('row', 'col'), may hold values from 0 to 15
- pair_b: int32 [3072, 192], P('row', 'col'), may hold values from 0 to 16, as said below
- owner: int32 [18432, 1], P(('row', 'col')), may hold values from 0 to 11; in each aligned block of 24 rows (0 to 23, 24 to 47, ...) at most 4 rows name the same one
Outputs:
- owned: bfloat16 [36864, 128, 128], P(('row', 'col'))
The draws below stay inside these ranges and needn't reach their ends.
Inputs may be any that keep to these rules, and one draw needn't show every extreme that they name: `pair_b`: entries equal to 16 are padding. In each product block and step the live pairs come first, at least one, and are distinct; some block of every device and step has all 16 live and some has padding. Among the 24 blocks of one device no owner is named more than 4 times.
All inputs are finite; a program needn't handle non-finite values.
Results may differ from the reference program's by a relative error of at most 0.0012.
Values may be sent and summed in bfloat16 or wider, within the bound.
No kernel may reach another device: no remote copies, remote signals or barrier semaphores. Data moves between devices by JAX's collectives and lax.ppermute only.
A program may use at most 64 MiB of HBM per device.

```python
import math
import jax
import jax.numpy as jnp
import numpy as np
from jax import lax

BS = 128
NA = 16
NB = 16
KP = 16
STEPS = 2
NCS = 24
CAP = 4
N_ROW = 64
N_COL = 12


def draw_pair_b(key, part):
    key = jax.random.fold_in(key, 7)
    key_count, key_first = jax.random.split(key)
    row_count = N_ROW * STEPS * NCS
    live_count = jax.random.randint(key_count, (row_count, N_COL, 1), 1, KP + 1)
    slot_index = (jnp.arange(row_count, dtype=jnp.int32) % NCS)[:, None, None]
    live_count = jnp.where(slot_index == 0, KP, jnp.where(slot_index == 1, KP - 1, live_count))
    first_pick = jax.random.randint(key_first, (row_count, N_COL, 1), 0, NB)
    position = jnp.arange(KP, dtype=jnp.int32)[None, None, :]
    chosen = (first_pick + position) % NB
    chosen = jnp.where(position < live_count, chosen, NB)
    return chosen.reshape(row_count, N_COL * KP).astype(jnp.int32)


def touch_ends(entries, own_key, smallest, high):
    index_at = [jax.random.randint(jax.random.fold_in(own_key, axis), (), 0, length) for axis, length in enumerate(entries.shape)]
    main_axis = entries.shape.index(max(entries.shape))
    next_to = index_at[:main_axis] + [(index_at[main_axis] + 1) % entries.shape[main_axis]] + index_at[main_axis + 1:]
    return entries.at[tuple(index_at)].set(smallest).at[tuple(next_to)].set(high)


def block_scale(stream_key, extent, shards, smallest, high):
    level = 1.0
    for axis_at, parts in shards:
        steps = jax.random.uniform(jax.random.fold_in(jax.random.fold_in(stream_key, 6), axis_at), (parts,), jnp.float32, smallest / len(shards), high / len(shards))
        level = level * jnp.repeat(jnp.exp(steps), extent[axis_at] // parts).reshape((-1,) + (1,) * (len(extent) - 1 - axis_at))
    return level


def shared_out(stream_key, own, number, rows, amount, top, limit, lean):
    sequence = jax.random.permutation(stream_key, amount)
    crowded, common = portions_of(amount, rows * top, limit, lean, True), portions_of(amount, rows * top, limit, lean, False)
    places = jnp.arange(amount)

    def named(sizes, offset_by):
        used = int((sizes > 0).sum())
        fixed = max(1, used // 4)
        shifted = fixed + (places - fixed + offset_by * (used - fixed)) % max(1, amount - fixed)
        return jnp.zeros((amount,), jnp.int32).at[sequence[jnp.where(places < fixed, places, shifted)]].set(jnp.asarray(sizes, jnp.int32))

    sizes = jnp.where(number % 4 == 0, named(crowded, number // 4), named(common, number - number // 4 - 1))
    mixed = jax.random.permutation(jax.random.fold_in(own, 3), amount)
    giver, receiver = mixed[0:amount // 2 * 2:2], mixed[1:amount // 2 * 2:2]
    room = jnp.minimum(sizes[giver] - 1, limit - sizes[receiver]) // 2
    room = jnp.where((giver == sequence[0]) | (receiver == sequence[0]) | (sizes[receiver] == 0), 0, jnp.maximum(room, 0))
    shifted = jax.random.randint(jax.random.fold_in(own, 4), (amount // 2,), 0, 1 << 20) % (room + 1)
    sizes = sizes.at[giver].add(-shifted).at[receiver].add(shifted)
    members = jnp.searchsorted(jnp.cumsum(sizes), jnp.arange(rows * top), side="right").astype(jnp.int32)
    table = members.reshape(top, rows).T
    table = table[jax.random.permutation(jax.random.fold_in(own, 1), rows)]
    offset_by = jax.random.randint(jax.random.fold_in(own, 2), (rows, 1), 0, top)
    return jnp.take_along_axis(table, (jnp.arange(top)[None, :] + offset_by) % top, axis=1)


def portions_of(number_of, total, most, lean, full):
    weights = [(1 << 20) // math.isqrt(standing ** lean) + 1 for standing in range(1, number_of + 1)]
    largest = most if full else min(most, max(-(-total // number_of), total * weights[0] // sum(weights)))
    least = 1 if total - largest >= number_of - 1 else 0
    counts, rest = [largest] + [least] * (number_of - 1), total - largest - least * (number_of - 1)
    while rest > 0:
        candidates = [i for i in range(1, number_of) if counts[i] < largest] or [i for i in range(1, number_of) if counts[i] < most]
        pool, left = sum([weights[i] for i in candidates]), rest
        for i in candidates:
            extra = min(most - counts[i], max(1, left * weights[i] // pool), rest)
            counts[i] = counts[i] + extra
            rest = rest - extra
    return np.array(counts)


def gaussian(rng, shape, scale, reach, shards=(), kind=jnp.bfloat16):
    entries = scale * jax.random.normal(rng, shape, jnp.float32)
    if shards:
        entries = entries * block_scale(rng, shape, shards, -0.22, 0.18)
    return jnp.clip(entries, -reach, reach).astype(kind)


def setup_inputs(seed: int = 0) -> dict:
    seeds = jax.random.split(jax.random.key(seed), 6)
    a_blocks = gaussian(seeds[0], (N_ROW * NA, N_COL * BS, BS), 1.0, 6.0, ((0, 64), (1, 12)))
    b_blocks = gaussian(seeds[1], (N_ROW * NB, N_COL * BS, BS), (KP * BS) ** -0.5, 0.125, ((0, 64), (1, 12)))
    pair_a = touch_ends(jax.random.randint(seeds[2], (N_ROW * STEPS * NCS, N_COL * KP), 0, NA), jax.random.fold_in(seeds[2], 1), 0, NA - 1).astype(jnp.int32)
    pair_b = draw_pair_b(jax.random.fold_in(seeds[5], 71), 0)
    owner_keys = jax.random.split(jax.random.fold_in(seeds[4], 1), (N_ROW * N_COL * NCS) // NCS)
    owner_turns = jax.random.permutation(jax.random.fold_in(seeds[4], 3), (N_ROW * N_COL * NCS) // NCS)
    owner = jax.vmap(lambda own, number: shared_out(jax.random.fold_in(seeds[4], 2), own, number, NCS, N_COL, 1, CAP, 2))(owner_keys, owner_turns).reshape((N_ROW * N_COL * NCS, 1))
    return dict(a_blocks=a_blocks, b_blocks=b_blocks, pair_a=pair_a, pair_b=pair_b, owner=owner)


def block_products(a_panel, b_panel, picks_a, picks_b):
    right_ext = jnp.concatenate([b_panel, jnp.zeros((1,) + b_panel.shape[1:], b_panel.dtype)], 0)
    left_batch = a_panel[picks_a].astype(jnp.float32)
    right_batch = right_ext[picks_b].astype(jnp.float32)
    return lax.dot_general(left_batch, right_batch, (((1, 3), (1, 2)), ((0,), (0,))))


def reference(a_blocks, b_blocks, pair_a, pair_b, owner):
    a_grid = a_blocks.reshape(N_ROW, NA, N_COL, BS, BS)
    b_grid = b_blocks.reshape(N_ROW, NB, N_COL, BS, BS)
    picks_a_all = pair_a.reshape(N_ROW, STEPS, NCS, N_COL, KP)
    picks_b_all = pair_b.reshape(N_ROW, STEPS, NCS, N_COL, KP)

    def one_device(device):
        row_index = device // N_COL
        col_index = device % N_COL
        summed = jnp.zeros((NCS, BS, BS), jnp.float32)
        for step_index in range(STEPS):
            a_panel = a_grid[row_index, :, step_index]
            b_panel = b_grid[step_index, :, col_index]
            picks_a = picks_a_all[row_index, step_index, :, col_index]
            picks_b = picks_b_all[row_index, step_index, :, col_index]
            summed = summed + block_products(a_panel, b_panel, picks_a, picks_b)
        return summed.astype(jnp.bfloat16)

    blocks = lax.map(one_device, jnp.arange(N_ROW * N_COL, dtype=jnp.int32))
    owners = owner.reshape(N_ROW, N_COL, NCS)
    matches = (owners[..., None] == jnp.arange(N_COL, dtype=jnp.int32)).astype(jnp.int32)
    order_rank = jnp.sum((jnp.cumsum(matches, axis=2) - matches) * matches, axis=3).astype(jnp.int32)
    row_ids = jnp.broadcast_to(jnp.arange(N_ROW, dtype=jnp.int32)[:, None, None], owners.shape)
    col_ids = jnp.broadcast_to(jnp.arange(N_COL, dtype=jnp.int32)[None, :, None], owners.shape)
    result = jnp.zeros((N_ROW, N_COL, N_COL, CAP, BS, BS), jnp.bfloat16)
    result = result.at[row_ids, owners, col_ids, order_rank].set(blocks.reshape(N_ROW, N_COL, NCS, BS, BS))
    return result.reshape(N_ROW * N_COL * N_COL * CAP, BS, BS)
```

```python
import functools

import jax
import jax.numpy as jnp
from jax import lax
from jax.experimental import pallas as pl
from jax.experimental.pallas import tpu as pltpu
from jax.sharding import PartitionSpec as P

BS = 128
KP = 16
STEPS = 2
NB = 16
CAP = 4
N_COL = 12
HELD = 3
APART = N_COL // HELD
QUARTER = NB // 4


def signed(hop):
    hop = hop % N_COL
    return hop if hop <= N_COL // 2 else hop - N_COL


def plan_routes():
    chosen, ties = {}, 0
    for apart in range(N_COL):
        options = [(abs(signed(apart + g * APART)), signed(apart + g * APART), g) for g in range(HELD)]
        least = min(o[0] for o in options)
        near = [o for o in options if o[0] == least]
        if len(near) > 1:
            near = [o for o in near if (o[1] > 0) == (ties % 2 == 0)]
            ties += 1
        chosen[apart] = near[0][1:]
    hops = sorted({h for h, _ in chosen.values()}, key=lambda h: (-abs(h), h))
    routes, base, at = {}, {}, 0
    for h in hops:
        routes[h] = sorted(g for hop, g in chosen.values() if hop == h)
        for g in routes[h]:
            apart = (h - g * APART) % N_COL
            base[apart] = (g, at)
            at += CAP
    return routes, base


ROUTES, BASE = plan_routes()
FIRST = {h: sum(CAP * len(v) for k, v in list(ROUTES.items())[: list(ROUTES).index(h)]) for h in ROUTES}


def product_kernel(hops, place, source, picks_a, picks_b, own, from_low, from_high, right_own, right_other, *rest):
    outs, left_all = rest[:-1], rest[-1]
    kind, core = place[0], place[1]

    @pl.when(kind == 0)
    def _():
        left_all[0:NB] = own[...]
        left_all[NB : 2 * NB] = from_high[...]

    @pl.when(kind == 1)
    def _():
        left_all[0:NB] = from_low[...]
        left_all[NB : 2 * NB] = own[...]

    @pl.when(kind == 2)
    def _():
        left_all[0:NB] = from_high[...]
        left_all[NB : 2 * NB] = from_low[...]

    left_all[2 * NB] = jnp.zeros((BS, BS), left_all.dtype)

    def fill(rights):
        for out, hop in zip(outs, hops):

            def one_slot(i, carry, out=out, first=FIRST[hop]):
                at = source[first + i]

                @pl.when(at >= 0)
                def _():
                    total = None
                    for s in range(STEPS):
                        left = [left_all[picks_a[at, s * KP + k]] for k in range(KP)]
                        right = [rights[s][picks_b[at, s * KP + k]] for k in range(KP)]
                        part = jnp.dot(
                            jnp.concatenate(left, 1), jnp.concatenate(right, 0), preferred_element_type=jnp.float32
                        )
                        total = part if total is None else total + part
                    out[i] = total.astype(out.dtype)

                @pl.when(at < 0)
                def _():
                    out[i] = jnp.zeros((BS, BS), out.dtype)

                return carry

            lax.fori_loop(0, out.shape[0], one_slot, 0)

    @pl.when(core == 0)
    def _():
        fill((right_own, right_other))

    @pl.when(core == 1)
    def _():
        fill((right_other, right_own))


def place_kernel(at, *refs):
    arrived, out = refs[:-1], refs[-1]
    for ref, (hop, held) in zip(arrived, ROUTES.items()):
        for n, g in enumerate(held):
            column = lax.rem(at[0] - hop + g * APART + 2 * N_COL, N_COL)
            out[pl.ds(column * CAP, CAP)] = ref[n * CAP : (n + 1) * CAP]


def shift(value, axis, size, hop):
    return lax.ppermute(value, axis, [(i, (i + hop) % size) for i in range(size)])


def x_shift(value, hop):
    return lax.ppermute(
        value, "row", [(8 * y + 2 * x + q, 8 * y + 2 * ((x - hop) % 4) + q) for y in range(8) for x in range(4) for q in range(2)]
    )


def spread_chunk(b_blocks, row):
    got = [
        lax.ppermute(b_blocks[x * QUARTER : (x + 1) * QUARTER], "row", [(0, 2 * x), (1, 2 * x + 1)]) for x in range(1, 4)
    ]
    chunk = b_blocks[0:QUARTER]
    for x in range(1, 4):
        chunk = jnp.where((row // 2) % 4 == x, got[x - 1], chunk)
    y_at = row // 8
    for hops in (((0, 3),), ((0, 5),)), (((0, 1), (3, 4), (5, 6)), ((0, 7), (3, 2))):
        got = [lax.ppermute(chunk, "row", [(8 * a + k, 8 * b + k) for a, b in pairs for k in range(8)]) for pairs in hops]
        for pairs, part in zip(hops, got):
            reached = functools.reduce(jnp.logical_or, [y_at == b for _, b in pairs])
            chunk = jnp.where(reached, part, chunk)
    return chunk


def spread(a_blocks, b_blocks, plan, row, col):
    third = col // 3
    near = lax.ppermute(a_blocks, "col", [(0, 3), (1, 4)])
    far = lax.ppermute(a_blocks, "col", [(0, 9), (1, 10)])
    chunk = spread_chunk(b_blocks, row)
    sent = jnp.concatenate([chunk.reshape(QUARTER * BS, BS), plan], 0)
    came = [shift(sent, "col", N_COL, -g * APART) for g in range(1, HELD)]
    held = jnp.concatenate([chunk] + [c[: QUARTER * BS].reshape(QUARTER, BS, BS) for c in came], 0)
    plans = [plan] + [c[QUARTER * BS :] for c in came]
    own = jnp.where(third == 1, near, jnp.where(third == 3, far, a_blocks))
    held, own = lax.optimization_barrier((held, own))

    after, behind = x_shift(held, 1), x_shift(held, 3)
    half = HELD * QUARTER // 2
    low = lax.ppermute(own[: NB // 2], "col", [(3, 6), (4, 7)])
    high = lax.ppermute(own[NB // 2 :], "col", [(9, 6), (10, 7)])
    own = jnp.where(third == 2, jnp.concatenate([low, high], 0), own)
    after, behind, own = lax.optimization_barrier((after, behind, own))

    across = [x_shift(after[:half], 1), x_shift(behind[half:], 3)]
    from_low = lax.ppermute(own, "col", [(z, (z + 1) % 12) for z in range(12) if z % 3 < 2])
    from_high = lax.ppermute(own, "col", [(z, (z - 1) % 12) for z in range(12) if z % 3 < 2])
    right_own = jnp.concatenate([held, after] + across + [behind], 0)
    right_other = lax.ppermute(right_own, "row", [(i, i ^ 1) for i in range(64)])
    return plans, own, from_low, from_high, right_own, right_other


def on_device(a_blocks, b_blocks, pair_a, pair_b, owner):
    n_slots = owner.shape[0]
    row = lax.axis_index("row")
    col = lax.axis_index("col")
    x_at, core = (row // 2) % 4, row % 2

    plan = jnp.concatenate(
        [pair_a[:n_slots], pair_a[n_slots:], pair_b[:n_slots], pair_b[n_slots:], owner], axis=1
    ).astype(jnp.bfloat16)
    plan = jnp.pad(plan, ((0, 32 - n_slots), (0, BS - plan.shape[1])))
    plans, own, from_low, from_high, right_own, right_other = spread(a_blocks, b_blocks, plan, row, col)
    slots, picks_a, picks_b = [], [], []
    for g, plan in enumerate(plans):
        plan = plan[:n_slots].astype(jnp.int32)
        owners = plan[:, 4 * KP]
        before = jnp.arange(n_slots)[None, :] < jnp.arange(n_slots)[:, None]
        rank = jnp.sum(((owners[:, None] == owners[None, :]) & before).astype(jnp.int32), axis=1)
        apart = (owners - col - g * APART + 2 * N_COL) % N_COL
        start = jnp.full((n_slots,), -N_COL * CAP, jnp.int32)
        for e, (index, at) in BASE.items():
            if index == g:
                start = jnp.where(apart == e, at, start)
        slots.append(start + rank)
        step = (jnp.arange(2 * KP, dtype=jnp.int32) // KP)[None, :]
        block = plan[:, 2 * KP : 4 * KP]
        live = block < NB
        picks_a.append(jnp.where(live, plan[:, : 2 * KP] + step * NB, 2 * NB))
        where = ((block // QUARTER - x_at + 4) % 4) * (HELD * QUARTER) + g * QUARTER + block % QUARTER
        picks_b.append(jnp.where(live, where, 0))
    slots = jnp.concatenate(slots)
    picks_a = jnp.concatenate(picks_a)
    picks_b = jnp.concatenate(picks_b)
    hit = slots[None, :] == jnp.arange(N_COL * CAP, dtype=jnp.int32)[:, None]
    source = jnp.max(jnp.where(hit, jnp.arange(HELD * n_slots, dtype=jnp.int32)[None, :], -1), axis=1)

    smem, vmem = pl.BlockSpec(memory_space=pltpu.SMEM), pl.BlockSpec(memory_space=pltpu.VMEM)

    def products(hops):
        count = sum(CAP * len(ROUTES[h]) for h in hops)
        return pl.pallas_call(
            functools.partial(product_kernel, hops),
            out_shape=[jax.ShapeDtypeStruct((CAP * len(ROUTES[h]), BS, BS), jnp.bfloat16) for h in hops],
            in_specs=[smem] * 4 + [vmem] * 5,
            out_specs=[vmem] * len(hops),
            scratch_shapes=[pltpu.VMEM((2 * NB + 1, BS, BS), jnp.bfloat16)],
            compiler_params=pltpu.CompilerParams(vmem_limit_bytes=24 * 2**20),
            cost_estimate=pl.CostEstimate(flops=count * 2 * KP * BS**3, bytes_accessed=4 * 2**20, transcendentals=0),
            name="products",
        )(jnp.stack([col % 3, core]), source, picks_a, picks_b, own, from_low, from_high, right_own, right_other)

    far = tuple(h for h in ROUTES if h != 0)
    made = list(products(far)) + list(products((0,)))
    arrived = [part if hop == 0 else shift(part, "col", N_COL, hop) for part, hop in zip(made, ROUTES)]
    return pl.pallas_call(
        place_kernel,
        out_shape=jax.ShapeDtypeStruct((N_COL * CAP, BS, BS), jnp.bfloat16),
        in_specs=[smem] + [vmem] * len(ROUTES),
        out_specs=vmem,
        compiler_params=pltpu.CompilerParams(vmem_limit_bytes=16 * 2**20),
        name="arrivals",
    )(jnp.full((1,), col, jnp.int32), *arrived)


def solution(mesh):
    return jax.shard_map(
        on_device,
        mesh=mesh,
        in_specs=(
            P("row", "col", None),
            P("row", "col", None),
            P("row", "col"),
            P("row", "col"),
            P(("row", "col"), None),
        ),
        out_specs=P(("row", "col"), None, None),
        check_vma=False,
    )
```

```python
import functools

import jax
import jax.numpy as jnp
from jax import lax
from jax.experimental import pallas as pl
from jax.experimental.pallas import tpu as pltpu
from jax.sharding import PartitionSpec as P

BS = 128
KP = 16
STEPS = 2
NB = 16
CAP = 4
N_COL = 12
HELD = 3
APART = N_COL // HELD
QUARTER = NB // 4
SLOTS = 24
TOGETHER = 3


def signed(hop):
    hop = hop % N_COL
    return hop if hop <= N_COL // 2 else hop - N_COL


def plan_routes():
    chosen, ties = {}, 0
    for apart in range(N_COL):
        options = [(abs(signed(apart + g * APART)), signed(apart + g * APART), g) for g in range(HELD)]
        least = min(o[0] for o in options)
        near = [o for o in options if o[0] == least]
        if len(near) > 1:
            near = [o for o in near if (o[1] > 0) == (ties % 2 == 0)]
            ties += 1
        chosen[apart] = near[0][1:]
    hops = sorted({h for h, _ in chosen.values()}, key=lambda h: (-abs(h), h))
    routes, base, at = {}, {}, 0
    for h in hops:
        routes[h] = sorted(g for hop, g in chosen.values() if hop == h)
        for g in routes[h]:
            apart = (h - g * APART) % N_COL
            base[apart] = (g, at)
            at += CAP
    return routes, base


ROUTES, BASE = plan_routes()
FIRST = {h: sum(CAP * len(v) for k, v in list(ROUTES.items())[: list(ROUTES).index(h)]) for h in ROUTES}


def product_kernel(hops, table, own, from_low, from_high, right_own, right_other, *rest):
    outs, left_all = rest[:-1], rest[-1]
    notes = HELD * SLOTS
    kind, core = table[notes, 0], table[notes, 1]

    @pl.when(kind == 0)
    def _():
        left_all[0:NB] = own[...]
        left_all[NB : 2 * NB] = from_high[...]

    @pl.when(kind == 1)
    def _():
        left_all[0:NB] = from_low[...]
        left_all[NB : 2 * NB] = own[...]

    @pl.when(kind == 2)
    def _():
        left_all[0:NB] = from_high[...]
        left_all[NB : 2 * NB] = from_low[...]

    left_all[2 * NB] = jnp.zeros((BS, BS), left_all.dtype)

    def one_block(rights, at):
        total = None
        for s in range(STEPS):
            left = [left_all[table[at, s * KP + k]] for k in range(KP)]
            right = [rights[s][table[at, (STEPS + s) * KP + k]] for k in range(KP)]
            part = jnp.dot(jnp.concatenate(left, 1), jnp.concatenate(right, 0), preferred_element_type=jnp.float32)
            total = part if total is None else total + part
        return total

    def fill(rights):
        for out, hop in zip(outs, hops):

            number, first = table[notes, 2 + list(ROUTES).index(hop)], FIRST[hop]
            out[...] = jnp.zeros_like(out)

            def some_slots(i, carry, out=out, number=number, first=first):
                places = [first + jnp.minimum(TOGETHER * i + u, number - 1) for u in range(TOGETHER)]
                sums = [one_block(rights, table[notes + 2, p]) for p in places]
                for p, total in zip(places, sums):
                    out[table[notes + 1, p]] = total.astype(out.dtype)
                return carry

            lax.fori_loop(0, (number + TOGETHER - 1) // TOGETHER, some_slots, 0)

    @pl.when(core == 0)
    def _():
        fill((right_own, right_other))

    @pl.when(core == 1)
    def _():
        fill((right_other, right_own))


def place_kernel(at, *refs):
    arrived, out = refs[:-1], refs[-1]
    for ref, (hop, held) in zip(arrived, ROUTES.items()):
        for n, g in enumerate(held):
            column = lax.rem(at[0] - hop + g * APART + 2 * N_COL, N_COL)
            out[pl.ds(column * CAP, CAP)] = ref[n * CAP : (n + 1) * CAP]


def join_kernel(third, own, low, high, out):
    @pl.when(third[0] == 2)
    def _():
        out[0 : NB // 2] = low[...]
        out[NB // 2 :] = high[...]

    @pl.when(third[0] != 2)
    def _():
        out[...] = own[...]


def shift(value, axis, size, hop):
    return lax.ppermute(value, axis, [(i, (i + hop) % size) for i in range(size)])


def x_shift(value, hop):
    return lax.ppermute(
        value, "row", [(8 * y + 2 * x + q, 8 * y + 2 * ((x - hop) % 4) + q) for y in range(8) for x in range(4) for q in range(2)]
    )


def spread_chunk(quarters, row):
    got = [lax.ppermute(quarters[x], "row", [(0, 2 * x), (1, 2 * x + 1)]) for x in range(1, 4)]
    chunk = quarters[0]
    for x in range(1, 4):
        chunk = jnp.where((row // 2) % 4 == x, got[x - 1], chunk)
    y_at = row // 8
    for hops in (((0, 3),), ((0, 5),)), (((0, 1), (3, 4), (5, 6)), ((0, 7), (3, 2))):
        got = [lax.ppermute(chunk, "row", [(8 * a + k, 8 * b + k) for a, b in pairs for k in range(8)]) for pairs in hops]
        for pairs, part in zip(hops, got):
            reached = functools.reduce(jnp.logical_or, [y_at == b for _, b in pairs])
            chunk = jnp.where(reached, part, chunk)
    return chunk


def spread(a_blocks, b_blocks, plan, row, col):
    third = col // 3
    quarters = [b_blocks[x * QUARTER : (x + 1) * QUARTER] for x in range(4)]
    near = lax.ppermute(a_blocks, "col", [(0, 3), (1, 4)])
    far = lax.ppermute(a_blocks, "col", [(0, 9), (1, 10)])
    chunk = spread_chunk(quarters, row)
    sent = jnp.concatenate([chunk.reshape(QUARTER * BS, BS), plan], 0)
    came = [shift(sent, "col", N_COL, -g * APART) for g in range(1, HELD)]
    held = jnp.concatenate([chunk] + [c[: QUARTER * BS].reshape(QUARTER, BS, BS) for c in came], 0)
    plans = [plan] + [c[QUARTER * BS :] for c in came]
    own = jnp.where(third == 1, near, jnp.where(third == 3, far, a_blocks))
    low = lax.ppermute(own[: NB // 2], "col", [(3, 6), (4, 7)])
    high = lax.ppermute(own[NB // 2 :], "col", [(9, 6), (10, 7)])
    own = pl.pallas_call(
        join_kernel,
        out_shape=jax.ShapeDtypeStruct(own.shape, own.dtype),
        in_specs=[pl.BlockSpec(memory_space=pltpu.SMEM)] + [pl.BlockSpec(memory_space=pltpu.VMEM)] * 3,
        out_specs=pl.BlockSpec(memory_space=pltpu.VMEM),
        compiler_params=pltpu.CompilerParams(vmem_limit_bytes=8 * 2**20),
        cost_estimate=pl.CostEstimate(flops=10**10, bytes_accessed=2**20, transcendentals=0),
        name="join",
    )(jnp.full((1,), third, jnp.int32), own, low, high)

    after, behind = x_shift(held, 1), x_shift(held, 3)
    after, behind, own = lax.optimization_barrier((after, behind, own))
    half = HELD * QUARTER // 2
    from_low = lax.ppermute(own, "col", [(z, (z + 1) % 12) for z in range(12) if z % 3 < 2])
    from_high = lax.ppermute(own, "col", [(z, (z - 1) % 12) for z in range(12) if z % 3 < 2])
    across = [x_shift(after[:half], 1), x_shift(behind[half:], 3)]
    right_own = jnp.concatenate([held, after] + across + [behind], 0)
    right_own, from_low, from_high = lax.optimization_barrier((right_own, from_low, from_high))
    right_other = lax.ppermute(right_own, "row", [(i, i ^ 1) for i in range(64)])
    return plans, own, from_low, from_high, right_own, right_other


def on_device(a_blocks, b_blocks, pair_a, pair_b, owner):
    n_slots = owner.shape[0]
    row = lax.axis_index("row")
    col = lax.axis_index("col")
    x_at, core = (row // 2) % 4, row % 2

    plan = jnp.concatenate(
        [pair_a[:n_slots], pair_a[n_slots:], pair_b[:n_slots], pair_b[n_slots:], owner], axis=1
    ).astype(jnp.bfloat16)
    plan = jnp.pad(plan, ((0, 32 - n_slots), (0, BS - plan.shape[1])))
    plans, own, from_low, from_high, right_own, right_other = spread(a_blocks, b_blocks, plan, row, col)
    slots, picks = [], []
    for g, plan in enumerate(plans):
        plan = plan[:n_slots].astype(jnp.int32)
        owners = plan[:, 4 * KP]
        before = jnp.arange(n_slots)[None, :] < jnp.arange(n_slots)[:, None]
        rank = jnp.sum(((owners[:, None] == owners[None, :]) & before).astype(jnp.int32), axis=1)
        apart = (owners - col - g * APART + 2 * N_COL) % N_COL
        start = jnp.full((n_slots,), -N_COL * CAP, jnp.int32)
        for e, (index, at) in BASE.items():
            if index == g:
                start = jnp.where(apart == e, at, start)
        slots.append(start + rank)
        step = (jnp.arange(2 * KP, dtype=jnp.int32) // KP)[None, :]
        block = plan[:, 2 * KP : 4 * KP]
        live = block < NB
        left = jnp.where(live, plan[:, : 2 * KP] + step * NB, 2 * NB)
        where = ((block // QUARTER - x_at + 4) % 4) * (HELD * QUARTER) + g * QUARTER + block % QUARTER
        picks.append(jnp.concatenate([left, jnp.where(live, where, 0)], 1))
    slots = jnp.concatenate(slots)
    hit = slots[None, :] == jnp.arange(N_COL * CAP, dtype=jnp.int32)[:, None]
    source = jnp.max(jnp.where(hit, jnp.arange(HELD * n_slots, dtype=jnp.int32)[None, :], -1), axis=1)
    group = jnp.concatenate([jnp.full((CAP * len(ROUTES[h]),), n, jnp.int32) for n, h in enumerate(ROUTES)])
    base = jnp.concatenate([jnp.full((CAP * len(ROUTES[h]),), FIRST[h], jnp.int32) for h in ROUTES])
    index = jnp.arange(N_COL * CAP, dtype=jnp.int32)
    filled = source >= 0
    ahead = (group[:, None] == group[None, :]) & (index[None, :] < index[:, None]) & filled[None, :]
    position = base + jnp.sum(ahead.astype(jnp.int32), axis=1)
    named = (position[None, :] == index[:, None]) & filled[None, :]
    slot_of = jnp.sum(jnp.where(named, (index - base)[None, :], 0), axis=1)
    row_of = jnp.sum(jnp.where(named, source[None, :], 0), axis=1)
    here = (group[None, :] == jnp.arange(len(ROUTES), dtype=jnp.int32)[:, None]) & filled[None, :]
    counts = jnp.sum(here.astype(jnp.int32), axis=1)
    notes = [jnp.concatenate([jnp.stack([col % 3, core]), counts]), slot_of, row_of]
    notes = jnp.stack([jnp.pad(n, (0, BS - n.shape[0])) for n in notes])
    table = jnp.concatenate([jnp.pad(jnp.concatenate(picks), ((0, 0), (0, BS - 4 * KP))), notes])

    smem, vmem = pl.BlockSpec(memory_space=pltpu.SMEM), pl.BlockSpec(memory_space=pltpu.VMEM)

    def products(hops):
        count = sum(CAP * len(ROUTES[h]) for h in hops)
        return pl.pallas_call(
            functools.partial(product_kernel, hops),
            out_shape=[jax.ShapeDtypeStruct((CAP * len(ROUTES[h]), BS, BS), jnp.bfloat16) for h in hops],
            in_specs=[smem] + [vmem] * 5,
            out_specs=[vmem] * len(hops),
            scratch_shapes=[pltpu.VMEM((2 * NB + 1, BS, BS), jnp.bfloat16)],
            compiler_params=pltpu.CompilerParams(vmem_limit_bytes=24 * 2**20),
            cost_estimate=pl.CostEstimate(flops=count * 2 * KP * BS**3, bytes_accessed=4 * 2**20, transcendentals=0),
            name="products",
        )(table, own, from_low, from_high, right_own, right_other)

    made = []
    for distance in sorted({abs(h) for h in ROUTES}, reverse=True):
        made += products(tuple(h for h in ROUTES if abs(h) == distance))
    arrived = [part if hop == 0 else shift(part, "col", N_COL, hop) for part, hop in zip(made, ROUTES)]
    return pl.pallas_call(
        place_kernel,
        out_shape=jax.ShapeDtypeStruct((N_COL * CAP, BS, BS), jnp.bfloat16),
        in_specs=[smem] + [vmem] * len(ROUTES),
        out_specs=vmem,
        compiler_params=pltpu.CompilerParams(vmem_limit_bytes=16 * 2**20),
        name="arrivals",
    )(jnp.full((1,), col, jnp.int32), *arrived)


def solution(mesh):
    return jax.shard_map(
        on_device,
        mesh=mesh,
        in_specs=(
            P("row", "col", None),
            P("row", "col", None),
            P("row", "col"),
            P("row", "col"),
            P(("row", "col"), None),
        ),
        out_specs=P(("row", "col"), None, None),
        check_vma=False,
    )
```

```python
import functools

import jax
import jax.numpy as jnp
from jax import lax
from jax.experimental import pallas as pl
from jax.experimental.pallas import tpu as pltpu
from jax.sharding import PartitionSpec as P

BS = 128
KP = 16
STEPS = 2
NB = 16
CAP = 4
N_COL = 12
HELD = 3
APART = N_COL // HELD
QUARTER = NB // 4
SLOTS = 24
TOGETHER = 3


def signed(hop):
    hop = hop % N_COL
    return hop if hop <= N_COL // 2 else hop - N_COL


def plan_routes():
    chosen, ties = {}, 0
    for apart in range(N_COL):
        options = [(abs(signed(apart + g * APART)), signed(apart + g * APART), g) for g in range(HELD)]
        least = min(o[0] for o in options)
        near = [o for o in options if o[0] == least]
        if len(near) > 1:
            near = [o for o in near if (o[1] > 0) == (ties % 2 == 0)]
            ties += 1
        chosen[apart] = near[0][1:]
    hops = sorted({h for h, _ in chosen.values()}, key=lambda h: (-abs(h), h))
    routes, base, at = {}, {}, 0
    for h in hops:
        routes[h] = sorted(g for hop, g in chosen.values() if hop == h)
        for g in routes[h]:
            apart = (h - g * APART) % N_COL
            base[apart] = (g, at)
            at += CAP
    return routes, base


ROUTES, BASE = plan_routes()
FIRST = {h: sum(CAP * len(v) for k, v in list(ROUTES.items())[: list(ROUTES).index(h)]) for h in ROUTES}


def product_kernel(hops, table, own, from_low, from_high, right_own, right_other, *rest):
    outs, left_all = rest[:-1], rest[-1]
    notes = HELD * SLOTS
    kind, core = table[notes, 0], table[notes, 1]

    @pl.when(kind == 0)
    def _():
        left_all[0:NB] = own[...]
        left_all[NB : 2 * NB] = from_high[...]

    @pl.when(kind == 1)
    def _():
        left_all[0:NB] = from_low[...]
        left_all[NB : 2 * NB] = own[...]

    @pl.when(kind == 2)
    def _():
        left_all[0:NB] = from_high[...]
        left_all[NB : 2 * NB] = from_low[...]

    left_all[2 * NB] = jnp.zeros((BS, BS), left_all.dtype)

    def one_block(rights, at):
        total = None
        for s in range(STEPS):
            left = [left_all[table[at, s * KP + k]] for k in range(KP)]
            right = [rights[s][table[at, (STEPS + s) * KP + k]] for k in range(KP)]
            part = jnp.dot(jnp.concatenate(left, 1), jnp.concatenate(right, 0), preferred_element_type=jnp.float32)
            total = part if total is None else total + part
        return total

    def fill(rights):
        for out, hop in zip(outs, hops):

            number, first = table[notes, 2 + list(ROUTES).index(hop)], FIRST[hop]
            out[...] = jnp.zeros_like(out)

            def some_slots(i, carry, out=out, number=number, first=first):
                places = [first + jnp.minimum(TOGETHER * i + u, number - 1) for u in range(TOGETHER)]
                sums = [one_block(rights, table[notes + 2, p]) for p in places]
                for p, total in zip(places, sums):
                    out[table[notes + 1, p]] = total.astype(out.dtype)
                return carry

            lax.fori_loop(0, (number + TOGETHER - 1) // TOGETHER, some_slots, 0)

    @pl.when(core == 0)
    def _():
        fill((right_own, right_other))

    @pl.when(core == 1)
    def _():
        fill((right_other, right_own))


def place_kernel(at, *refs):
    arrived, out = refs[:-1], refs[-1]
    for ref, (hop, held) in zip(arrived, ROUTES.items()):
        for n, g in enumerate(held):
            column = lax.rem(at[0] - hop + g * APART + 2 * N_COL, N_COL)
            out[pl.ds(column * CAP, CAP)] = ref[n * CAP : (n + 1) * CAP]


def join_kernel(third, own, low, high, out):
    @pl.when(third[0] == 2)
    def _():
        out[0 : NB // 2] = low[...]
        out[NB // 2 :] = high[...]

    @pl.when(third[0] != 2)
    def _():
        out[...] = own[...]


def shift(value, axis, size, hop):
    return lax.ppermute(value, axis, [(i, (i + hop) % size) for i in range(size)])


def x_shift(value, hop):
    return lax.ppermute(
        value, "row", [(8 * y + 2 * x + q, 8 * y + 2 * ((x - hop) % 4) + q) for y in range(8) for x in range(4) for q in range(2)]
    )


def spread_chunk(quarters, row):
    got = [lax.ppermute(quarters[x], "row", [(0, 2 * x), (1, 2 * x + 1)]) for x in range(1, 4)]
    chunk = quarters[0]
    for x in range(1, 4):
        chunk = jnp.where((row // 2) % 4 == x, got[x - 1], chunk)
    y_at = row // 8
    for hops in (((0, 3),), ((0, 5),)), (((0, 1), (3, 4), (5, 6)), ((0, 7), (3, 2))):
        got = [lax.ppermute(chunk, "row", [(8 * a + k, 8 * b + k) for a, b in pairs for k in range(8)]) for pairs in hops]
        for pairs, part in zip(hops, got):
            reached = functools.reduce(jnp.logical_or, [y_at == b for _, b in pairs])
            chunk = jnp.where(reached, part, chunk)
    return chunk


def spread(a_blocks, b_blocks, plan, row, col):
    third = col // 3
    quarters = [b_blocks[x * QUARTER : (x + 1) * QUARTER] for x in range(4)]
    near = lax.ppermute(a_blocks, "col", [(0, 3), (1, 4)])
    far = lax.ppermute(a_blocks, "col", [(0, 9), (1, 10)])
    chunk = spread_chunk(quarters, row)
    sent = jnp.concatenate([chunk.reshape(QUARTER * BS, BS), plan], 0)
    came = [shift(sent, "col", N_COL, -g * APART) for g in range(1, HELD)]
    held = jnp.concatenate([chunk] + [c[: QUARTER * BS].reshape(QUARTER, BS, BS) for c in came], 0)
    plans = [plan] + [c[QUARTER * BS :] for c in came]
    own = jnp.where(third == 1, near, jnp.where(third == 3, far, a_blocks))
    low = lax.ppermute(own[: NB // 2], "col", [(3, 6), (4, 7)])
    high = lax.ppermute(own[NB // 2 :], "col", [(9, 6), (10, 7)])
    own = pl.pallas_call(
        join_kernel,
        out_shape=jax.ShapeDtypeStruct(own.shape, own.dtype),
        in_specs=[pl.BlockSpec(memory_space=pltpu.SMEM)] + [pl.BlockSpec(memory_space=pltpu.VMEM)] * 3,
        out_specs=pl.BlockSpec(memory_space=pltpu.VMEM),
        compiler_params=pltpu.CompilerParams(vmem_limit_bytes=8 * 2**20),
        cost_estimate=pl.CostEstimate(flops=10**10, bytes_accessed=2**20, transcendentals=0),
        name="join",
    )(jnp.full((1,), third, jnp.int32), own, low, high)

    after, behind = x_shift(held, 1), x_shift(held, 3)
    half = HELD * QUARTER // 2
    from_low = lax.ppermute(own, "col", [(z, (z + 1) % 12) for z in range(12) if z % 3 < 2])
    from_high = lax.ppermute(own, "col", [(z, (z - 1) % 12) for z in range(12) if z % 3 < 2])
    across = [x_shift(after[:half], 1), x_shift(behind[half:], 3)]
    right_own = jnp.concatenate([held, after] + across + [behind], 0)
    right_own, from_low, from_high = lax.optimization_barrier((right_own, from_low, from_high))
    right_other = lax.ppermute(right_own, "row", [(i, i ^ 1) for i in range(64)])
    return plans, own, from_low, from_high, right_own, right_other


def on_device(a_blocks, b_blocks, pair_a, pair_b, owner):
    n_slots = owner.shape[0]
    row = lax.axis_index("row")
    col = lax.axis_index("col")
    x_at, core = (row // 2) % 4, row % 2

    plan = jnp.concatenate(
        [pair_a[:n_slots], pair_a[n_slots:], pair_b[:n_slots], pair_b[n_slots:], owner], axis=1
    ).astype(jnp.bfloat16)
    plan = jnp.pad(plan, ((0, 32 - n_slots), (0, BS - plan.shape[1])))
    plans, own, from_low, from_high, right_own, right_other = spread(a_blocks, b_blocks, plan, row, col)
    slots, picks = [], []
    for g, plan in enumerate(plans):
        plan = plan[:n_slots].astype(jnp.int32)
        owners = plan[:, 4 * KP]
        before = jnp.arange(n_slots)[None, :] < jnp.arange(n_slots)[:, None]
        rank = jnp.sum(((owners[:, None] == owners[None, :]) & before).astype(jnp.int32), axis=1)
        apart = (owners - col - g * APART + 2 * N_COL) % N_COL
        start = jnp.full((n_slots,), -N_COL * CAP, jnp.int32)
        for e, (index, at) in BASE.items():
            if index == g:
                start = jnp.where(apart == e, at, start)
        slots.append(start + rank)
        step = (jnp.arange(2 * KP, dtype=jnp.int32) // KP)[None, :]
        block = plan[:, 2 * KP : 4 * KP]
        live = block < NB
        left = jnp.where(live, plan[:, : 2 * KP] + step * NB, 2 * NB)
        where = ((block // QUARTER - x_at + 4) % 4) * (HELD * QUARTER) + g * QUARTER + block % QUARTER
        picks.append(jnp.concatenate([left, jnp.where(live, where, 0)], 1))
    slots = jnp.concatenate(slots)
    hit = slots[None, :] == jnp.arange(N_COL * CAP, dtype=jnp.int32)[:, None]
    source = jnp.max(jnp.where(hit, jnp.arange(HELD * n_slots, dtype=jnp.int32)[None, :], -1), axis=1)
    group = jnp.concatenate([jnp.full((CAP * len(ROUTES[h]),), n, jnp.int32) for n, h in enumerate(ROUTES)])
    base = jnp.concatenate([jnp.full((CAP * len(ROUTES[h]),), FIRST[h], jnp.int32) for h in ROUTES])
    index = jnp.arange(N_COL * CAP, dtype=jnp.int32)
    filled = source >= 0
    ahead = (group[:, None] == group[None, :]) & (index[None, :] < index[:, None]) & filled[None, :]
    position = base + jnp.sum(ahead.astype(jnp.int32), axis=1)
    named = (position[None, :] == index[:, None]) & filled[None, :]
    slot_of = jnp.sum(jnp.where(named, (index - base)[None, :], 0), axis=1)
    row_of = jnp.sum(jnp.where(named, source[None, :], 0), axis=1)
    here = (group[None, :] == jnp.arange(len(ROUTES), dtype=jnp.int32)[:, None]) & filled[None, :]
    counts = jnp.sum(here.astype(jnp.int32), axis=1)
    notes = [jnp.concatenate([jnp.stack([col % 3, core]), counts]), slot_of, row_of]
    notes = jnp.stack([jnp.pad(n, (0, BS - n.shape[0])) for n in notes])
    table = jnp.concatenate([jnp.pad(jnp.concatenate(picks), ((0, 0), (0, BS - 4 * KP))), notes])

    smem, vmem = pl.BlockSpec(memory_space=pltpu.SMEM), pl.BlockSpec(memory_space=pltpu.VMEM)

    def products(hops):
        count = sum(CAP * len(ROUTES[h]) for h in hops)
        return pl.pallas_call(
            functools.partial(product_kernel, hops),
            out_shape=[jax.ShapeDtypeStruct((CAP * len(ROUTES[h]), BS, BS), jnp.bfloat16) for h in hops],
            in_specs=[smem] + [vmem] * 5,
            out_specs=[vmem] * len(hops),
            scratch_shapes=[pltpu.VMEM((2 * NB + 1, BS, BS), jnp.bfloat16)],
            compiler_params=pltpu.CompilerParams(vmem_limit_bytes=24 * 2**20),
            cost_estimate=pl.CostEstimate(flops=count * 2 * KP * BS**3, bytes_accessed=4 * 2**20, transcendentals=0),
            name="products",
        )(table, own, from_low, from_high, right_own, right_other)

    away = tuple(h for h in ROUTES if h != 0)
    made = products(away) + products((0,))
    arrived = [part if hop == 0 else shift(part, "col", N_COL, hop) for part, hop in zip(made, ROUTES)]
    return pl.pallas_call(
        place_kernel,
        out_shape=jax.ShapeDtypeStruct((N_COL * CAP, BS, BS), jnp.bfloat16),
        in_specs=[smem] + [vmem] * len(ROUTES),
        out_specs=vmem,
        compiler_params=pltpu.CompilerParams(vmem_limit_bytes=16 * 2**20),
        name="arrivals",
    )(jnp.full((1,), col, jnp.int32), *arrived)


def solution(mesh):
    return jax.shard_map(
        on_device,
        mesh=mesh,
        in_specs=(
            P("row", "col", None),
            P("row", "col", None),
            P("row", "col"),
            P("row", "col"),
            P(("row", "col"), None),
        ),
        out_specs=P(("row", "col"), None, None),
        check_vma=False,
    )
```

```python
import functools

import jax
import jax.numpy as jnp
from jax import lax
from jax.experimental import pallas as pl
from jax.experimental.pallas import tpu as pltpu
from jax.sharding import PartitionSpec as P

BS = 128
KP = 16
STEPS = 2
NB = 16
CAP = 4
N_COL = 12
HELD = 3
APART = N_COL // HELD
QUARTER = NB // 4
SLOTS = 24
TOGETHER = 3


def signed(hop):
    hop = hop % N_COL
    return hop if hop <= N_COL // 2 else hop - N_COL


def plan_routes():
    chosen, ties = {}, 0
    for apart in range(N_COL):
        options = [(abs(signed(apart + g * APART)), signed(apart + g * APART), g) for g in range(HELD)]
        least = min(o[0] for o in options)
        near = [o for o in options if o[0] == least]
        if len(near) > 1:
            near = [o for o in near if (o[1] > 0) == (ties % 2 == 0)]
            ties += 1
        chosen[apart] = near[0][1:]
    hops = sorted({h for h, _ in chosen.values()}, key=lambda h: (-abs(h), h))
    routes, base, at = {}, {}, 0
    for h in hops:
        routes[h] = sorted(g for hop, g in chosen.values() if hop == h)
        for g in routes[h]:
            apart = (h - g * APART) % N_COL
            base[apart] = (g, at)
            at += CAP
    return routes, base


ROUTES, BASE = plan_routes()
FIRST = {h: sum(CAP * len(v) for k, v in list(ROUTES.items())[: list(ROUTES).index(h)]) for h in ROUTES}


def product_kernel(hops, table, own, from_low, from_high, right_own, right_other, *rest):
    outs, left_all = rest[:-1], rest[-1]
    notes = HELD * SLOTS
    kind, core = table[notes, 0], table[notes, 1]

    @pl.when(kind == 0)
    def _():
        left_all[0:NB] = own[...]
        left_all[NB : 2 * NB] = from_high[...]

    @pl.when(kind == 1)
    def _():
        left_all[0:NB] = from_low[...]
        left_all[NB : 2 * NB] = own[...]

    @pl.when(kind == 2)
    def _():
        left_all[0:NB] = from_high[...]
        left_all[NB : 2 * NB] = from_low[...]

    left_all[2 * NB] = jnp.zeros((BS, BS), left_all.dtype)

    def one_block(rights, at):
        total = None
        for s in range(STEPS):
            left = [left_all[table[at, s * KP + k]] for k in range(KP)]
            right = [rights[s][table[at, (STEPS + s) * KP + k]] for k in range(KP)]
            part = jnp.dot(jnp.concatenate(left, 1), jnp.concatenate(right, 0), preferred_element_type=jnp.float32)
            total = part if total is None else total + part
        return total

    def fill(rights):
        for out, hop in zip(outs, hops):

            number, first = table[notes, 2 + list(ROUTES).index(hop)], FIRST[hop]
            out[...] = jnp.zeros_like(out)

            def some_slots(i, carry, out=out, number=number, first=first):
                places = [first + jnp.minimum(TOGETHER * i + u, number - 1) for u in range(TOGETHER)]
                sums = [one_block(rights, table[notes + 2, p]) for p in places]
                for p, total in zip(places, sums):
                    out[table[notes + 1, p]] = total.astype(out.dtype)
                return carry

            lax.fori_loop(0, (number + TOGETHER - 1) // TOGETHER, some_slots, 0)

    @pl.when(core == 0)
    def _():
        fill((right_own, right_other))

    @pl.when(core == 1)
    def _():
        fill((right_other, right_own))


def place_kernel(at, *refs):
    arrived, out = refs[:-1], refs[-1]
    for ref, (hop, held) in zip(arrived, ROUTES.items()):
        for n, g in enumerate(held):
            column = lax.rem(at[0] - hop + g * APART + 2 * N_COL, N_COL)
            out[pl.ds(column * CAP, CAP)] = ref[n * CAP : (n + 1) * CAP]


def join_kernel(third, own, low, high, out):
    @pl.when(third[0] == 2)
    def _():
        out[0 : NB // 2] = low[...]
        out[NB // 2 :] = high[...]

    @pl.when(third[0] != 2)
    def _():
        out[...] = own[...]


def shift(value, axis, size, hop):
    return lax.ppermute(value, axis, [(i, (i + hop) % size) for i in range(size)])


def x_shift(value, hop):
    return lax.ppermute(
        value, "row", [(8 * y + 2 * x + q, 8 * y + 2 * ((x - hop) % 4) + q) for y in range(8) for x in range(4) for q in range(2)]
    )


def spread_chunk(quarters, row):
    got = [lax.ppermute(quarters[x], "row", [(0, 2 * x), (1, 2 * x + 1)]) for x in range(1, 4)]
    chunk = quarters[0]
    for x in range(1, 4):
        chunk = jnp.where((row // 2) % 4 == x, got[x - 1], chunk)
    y_at = row // 8
    for hops in (((0, 3),), ((0, 5),)), (((0, 1), (3, 4), (5, 6)), ((0, 7), (3, 2))):
        got = [lax.ppermute(chunk, "row", [(8 * a + k, 8 * b + k) for a, b in pairs for k in range(8)]) for pairs in hops]
        for pairs, part in zip(hops, got):
            reached = functools.reduce(jnp.logical_or, [y_at == b for _, b in pairs])
            chunk = jnp.where(reached, part, chunk)
    return chunk


def spread(a_blocks, b_blocks, plan, row, col):
    third = col // 3
    quarters = [b_blocks[x * QUARTER : (x + 1) * QUARTER] for x in range(4)]
    near = lax.ppermute(a_blocks, "col", [(0, 3), (1, 4)])
    far = lax.ppermute(a_blocks, "col", [(0, 9), (1, 10)])
    chunk = spread_chunk(quarters, row)
    sent = jnp.concatenate([chunk.reshape(QUARTER * BS, BS), plan], 0)
    came = [shift(sent, "col", N_COL, -g * APART) for g in range(1, HELD)]
    held = jnp.concatenate([chunk] + [c[: QUARTER * BS].reshape(QUARTER, BS, BS) for c in came], 0)
    plans = [plan] + [c[QUARTER * BS :] for c in came]
    own = jnp.where(third == 1, near, jnp.where(third == 3, far, a_blocks))
    low = lax.ppermute(own[: NB // 2], "col", [(3, 6), (4, 7)])
    high = lax.ppermute(own[NB // 2 :], "col", [(9, 6), (10, 7)])
    own = pl.pallas_call(
        join_kernel,
        out_shape=jax.ShapeDtypeStruct(own.shape, own.dtype),
        in_specs=[pl.BlockSpec(memory_space=pltpu.SMEM)] + [pl.BlockSpec(memory_space=pltpu.VMEM)] * 3,
        out_specs=pl.BlockSpec(memory_space=pltpu.VMEM),
        compiler_params=pltpu.CompilerParams(vmem_limit_bytes=8 * 2**20),
        cost_estimate=pl.CostEstimate(flops=10**10, bytes_accessed=2**20, transcendentals=0),
        name="join",
    )(jnp.full((1,), third, jnp.int32), own, low, high)

    after, behind, across = x_shift(held, 1), x_shift(held, 3), x_shift(held, 2)
    from_low = lax.ppermute(own, "col", [(z, (z + 1) % 12) for z in range(12) if z % 3 < 2])
    from_high = lax.ppermute(own, "col", [(z, (z - 1) % 12) for z in range(12) if z % 3 < 2])
    right_own = jnp.concatenate([held, after, across, behind], 0)
    right_own, from_low, from_high = lax.optimization_barrier((right_own, from_low, from_high))
    right_other = lax.ppermute(right_own, "row", [(i, i ^ 1) for i in range(64)])
    return plans, own, from_low, from_high, right_own, right_other


def on_device(a_blocks, b_blocks, pair_a, pair_b, owner):
    n_slots = owner.shape[0]
    row = lax.axis_index("row")
    col = lax.axis_index("col")
    x_at, core = (row // 2) % 4, row % 2

    plan = jnp.concatenate(
        [pair_a[:n_slots], pair_a[n_slots:], pair_b[:n_slots], pair_b[n_slots:], owner], axis=1
    ).astype(jnp.bfloat16)
    plan = jnp.pad(plan, ((0, 32 - n_slots), (0, BS - plan.shape[1])))
    plans, own, from_low, from_high, right_own, right_other = spread(a_blocks, b_blocks, plan, row, col)
    slots, picks = [], []
    for g, plan in enumerate(plans):
        plan = plan[:n_slots].astype(jnp.int32)
        owners = plan[:, 4 * KP]
        before = jnp.arange(n_slots)[None, :] < jnp.arange(n_slots)[:, None]
        rank = jnp.sum(((owners[:, None] == owners[None, :]) & before).astype(jnp.int32), axis=1)
        apart = (owners - col - g * APART + 2 * N_COL) % N_COL
        start = jnp.full((n_slots,), -N_COL * CAP, jnp.int32)
        for e, (index, at) in BASE.items():
            if index == g:
                start = jnp.where(apart == e, at, start)
        slots.append(start + rank)
        step = (jnp.arange(2 * KP, dtype=jnp.int32) // KP)[None, :]
        block = plan[:, 2 * KP : 4 * KP]
        live = block < NB
        left = jnp.where(live, plan[:, : 2 * KP] + step * NB, 2 * NB)
        where = ((block // QUARTER - x_at + 4) % 4) * (HELD * QUARTER) + g * QUARTER + block % QUARTER
        picks.append(jnp.concatenate([left, jnp.where(live, where, 0)], 1))
    slots = jnp.concatenate(slots)
    hit = slots[None, :] == jnp.arange(N_COL * CAP, dtype=jnp.int32)[:, None]
    source = jnp.max(jnp.where(hit, jnp.arange(HELD * n_slots, dtype=jnp.int32)[None, :], -1), axis=1)
    group = jnp.concatenate([jnp.full((CAP * len(ROUTES[h]),), n, jnp.int32) for n, h in enumerate(ROUTES)])
    base = jnp.concatenate([jnp.full((CAP * len(ROUTES[h]),), FIRST[h], jnp.int32) for h in ROUTES])
    index = jnp.arange(N_COL * CAP, dtype=jnp.int32)
    filled = source >= 0
    ahead = (group[:, None] == group[None, :]) & (index[None, :] < index[:, None]) & filled[None, :]
    position = base + jnp.sum(ahead.astype(jnp.int32), axis=1)
    named = (position[None, :] == index[:, None]) & filled[None, :]
    slot_of = jnp.sum(jnp.where(named, (index - base)[None, :], 0), axis=1)
    row_of = jnp.sum(jnp.where(named, source[None, :], 0), axis=1)
    here = (group[None, :] == jnp.arange(len(ROUTES), dtype=jnp.int32)[:, None]) & filled[None, :]
    counts = jnp.sum(here.astype(jnp.int32), axis=1)
    notes = [jnp.concatenate([jnp.stack([col % 3, core]), counts]), slot_of, row_of]
    notes = jnp.stack([jnp.pad(n, (0, BS - n.shape[0])) for n in notes])
    table = jnp.concatenate([jnp.pad(jnp.concatenate(picks), ((0, 0), (0, BS - 4 * KP))), notes])

    smem, vmem = pl.BlockSpec(memory_space=pltpu.SMEM), pl.BlockSpec(memory_space=pltpu.VMEM)

    def products(hops):
        count = sum(CAP * len(ROUTES[h]) for h in hops)
        return pl.pallas_call(
            functools.partial(product_kernel, hops),
            out_shape=[jax.ShapeDtypeStruct((CAP * len(ROUTES[h]), BS, BS), jnp.bfloat16) for h in hops],
            in_specs=[smem] + [vmem] * 5,
            out_specs=[vmem] * len(hops),
            scratch_shapes=[pltpu.VMEM((2 * NB + 1, BS, BS), jnp.bfloat16)],
            compiler_params=pltpu.CompilerParams(vmem_limit_bytes=24 * 2**20),
            cost_estimate=pl.CostEstimate(flops=count * 2 * KP * BS**3, bytes_accessed=4 * 2**20, transcendentals=0),
            name="products",
        )(table, own, from_low, from_high, right_own, right_other)

    away = tuple(h for h in ROUTES if h != 0)
    made = products(away) + products((0,))
    arrived = [part if hop == 0 else shift(part, "col", N_COL, hop) for part, hop in zip(made, ROUTES)]
    return pl.pallas_call(
        place_kernel,
        out_shape=jax.ShapeDtypeStruct((N_COL * CAP, BS, BS), jnp.bfloat16),
        in_specs=[smem] + [vmem] * len(ROUTES),
        out_specs=vmem,
        compiler_params=pltpu.CompilerParams(vmem_limit_bytes=16 * 2**20),
        name="arrivals",
    )(jnp.full((1,), col, jnp.int32), *arrived)


def solution(mesh):
    return jax.shard_map(
        on_device,
        mesh=mesh,
        in_specs=(
            P("row", "col", None),
            P("row", "col", None),
            P("row", "col"),
            P("row", "col"),
            P(("row", "col"), None),
        ),
        out_specs=P(("row", "col"), None, None),
        check_vma=False,
    )
```
